128 devices in a mesh: side: 2 (over core), grp: 64 (over x, y, z).
Axes of the slice: x: 4, y: 4, z: 4, core: 2. Of those that a mesh axis runs over, the one named last changes fastest.
Arguments:
- poles: float32 [65536], P(('side', 'grp')), may hold values from 0 to 1, as said below
- coupling: float32 [65536], P(('side', 'grp')), may hold values from -0.0234375 to 0.0234375
- kinds: int32 [65536], P(('side', 'grp')), may hold values from 0 to 3
- permutation: int32 [2, 32768], P('side'), may hold values from 0 to 32767, each once within a row
- block_map: int32 [2, 64, 2, 128], P('side', 'grp'), may hold values from 0 to 1, as said below
- left_vectors: bfloat16 [2, 12288, 32768], P('side', 'grp'), may hold values from -6 to 6
- right_vectors: bfloat16 [2, 12288, 32768], P('side', 'grp'), may hold values from -6 to 6
Outputs:
- new_left: bfloat16 [2, 12288, 256], P('side', 'grp')
- new_right: bfloat16 [2, 12288, 256], P('side', 'grp')
- root_offsets: float32 [256], replicated
The draws below stay inside these ranges and needn't reach their ends.
Inputs may be any that keep to these rules, and one draw needn't show every extreme that they name: Positive; the squares of any two poles differ by at least 0.4 / 65536; for every panel root r, pole_sq[r] < pole_sq[r + 1] and no pole's square lies strictly between them. `block_map`: each row of the last dimension (one child, row block and matrix) has at most 64 ones; some row has exactly 64. A zero marks a block whose entries are ignored.
All inputs are finite; a program needn't handle non-finite values.
Results may differ from the reference program's by a relative error of at most 0.008.
Values may be sent and summed in bfloat16 or wider, within the bound.
A program may use at most 192 MiB of HBM per device.

```python
import jax
import jax.numpy as jnp
from jax import lax

K = 65536
KH = 32768
P_SIZE = 128
NR = 256
BW = 256
NB = 128
MAXB = 64
ITERS = 8
R_DEV = 192
ROW_BLOCKS = 64
ROWS = 12288


def draw_poles(key, part):
    key = jax.random.fold_in(key, 11)
    jitter_key, first_key, second_key = jax.random.split(key, 3)
    half = K // 2
    chain = P_SIZE + 1
    margin = 2 * P_SIZE
    uniform_draw = jax.random.uniform(jitter_key, (K,), jnp.float32)
    jitter = 0.3 * (2.0 * uniform_draw - 1.0)
    first_start = jax.random.randint(first_key, (), margin, half - chain - margin + 1)
    second_start = jax.random.randint(second_key, (), half + margin, K - chain - margin + 1)
    ranks = jnp.arange(K, dtype=jnp.int32)
    in_first = (ranks >= first_start) & (ranks < first_start + chain)
    in_second = (ranks >= second_start) & (ranks < second_start + chain)
    near_first = (ranks >= first_start - margin) & (ranks < first_start) | (ranks >= first_start + chain) & (ranks < first_start + chain + margin)
    near_second = (ranks >= second_start - margin) & (ranks < second_start) | (ranks >= second_start + chain) & (ranks < second_start + chain + margin)
    in_chain = in_first | in_second
    mixed = jnp.logical_not(in_chain | near_first | near_second)
    mixed_order = jnp.cumsum(mixed.astype(jnp.int32)) - 1
    mixed_child = jnp.where(mixed_order < 2, 0, mixed_order % 2)
    child = jnp.where(near_first, 1, jnp.where(near_second, 0, mixed_child))
    free_slot = jnp.logical_not(in_chain)
    to_left = free_slot & (child == 0)
    to_right = free_slot & (child == 1)
    left_order = jnp.cumsum(to_left.astype(jnp.int32)) - 1
    right_order = jnp.cumsum(to_right.astype(jnp.int32)) - 1
    right_split = half - 2 * P_SIZE - 1
    right_index = jnp.where(right_order < right_split, half + 1 + right_order, K - P_SIZE + 1 + right_order - right_split)
    first_pos = ranks - first_start
    first_index = jnp.where(first_pos < P_SIZE, half - P_SIZE + first_pos, half)
    second_index = K - 2 * P_SIZE + (ranks - second_start)
    target = jnp.where(in_first, first_index, jnp.where(in_second, second_index, jnp.where(to_left, left_order, right_index)))
    rank_of_index = jnp.zeros((K,), jnp.int32).at[target].set(ranks)
    base = rank_of_index.astype(jnp.float32) + 0.5 + jitter
    return jnp.sqrt(base / K)


def draw_block_map(key, part):
    key = jax.random.fold_in(key, 23)
    map_rows = 4 * ROW_BLOCKS
    level_key, full_key, order_key = jax.random.split(key, 3)
    levels = jax.random.randint(level_key, (map_rows,), 0, 4)
    full_row = jax.random.randint(full_key, (), 0, map_rows)
    levels = jnp.where(jnp.arange(map_rows) == full_row, 0, levels)
    divisors = jnp.array([1, 2, 4, 8], jnp.int32)[levels]
    counts = MAXB // divisors
    row_keys = jax.random.split(order_key, map_rows)
    orders = jax.vmap(lambda each_key: jax.random.permutation(each_key, NB))(row_keys)
    flags = (orders < counts[:, None]).astype(jnp.int32)
    return flags.reshape(2, ROW_BLOCKS, 2, NB)


def plant(entries, rng, low, high):
    longest = entries.shape.index(max(entries.shape))
    spots = []
    for shift in (0, 1):
        where = [jax.random.randint(jax.random.fold_in(rng, axis), (), 0, length) for axis, length in enumerate(entries.shape)]
        where[longest] = (where[longest] + shift) % entries.shape[longest]
        spots.append(tuple(where))
    return entries.at[spots[0]].set(low).at[spots[1]].set(high)


def level_of(rng, shape, cuts, smallest, largest):
    loudness = 1.0
    for dim, shards_of in cuts:
        draws = jax.random.uniform(jax.random.fold_in(jax.random.fold_in(rng, 6), dim), (shards_of,), jnp.float32, smallest / len(cuts), largest / len(cuts))
        loudness = loudness * jnp.repeat(jnp.exp(draws), shape[dim] // shards_of).reshape((-1,) + (1,) * (len(shape) - 1 - dim))
    return loudness


def bell_draw(stream_key, extent, scale, most, cuts=(), held_as=jnp.bfloat16):
    drawn = scale * jax.random.normal(stream_key, extent, jnp.float32)
    if cuts:
        drawn = drawn * level_of(stream_key, extent, cuts, -0.22, 0.18)
    return jnp.clip(drawn, -most, most).astype(held_as)


def setup_inputs(seed: int = 0) -> dict:
    key_list = jax.random.split(jax.random.key(seed), 8)
    return {
        "poles": draw_poles(jax.random.fold_in(key_list[7], 71), 0),
        "coupling": bell_draw(key_list[1], (K,), K ** -0.5, 0.0234375, ((0, 128),), jnp.float32),
        "kinds": plant(jax.random.randint(key_list[2], (K,), 0, 4), jax.random.fold_in(key_list[2], 1), 0, 3).astype(jnp.int32),
        "permutation": jax.vmap(lambda own: jax.random.permutation(own, KH))(jax.random.split(key_list[3], 2)).reshape((2, KH)).astype(jnp.int32),
        "block_map": draw_block_map(jax.random.fold_in(key_list[7], 71), 0),
        "left_vectors": bell_draw(key_list[5], (2, ROWS, KH), 1.0, 6.0, ((0, 2), (1, 64))),
        "right_vectors": bell_draw(key_list[6], (2, ROWS, KH), 1.0, 6.0, ((0, 2), (1, 64))),
    }


def inverse_sums(pole_sq, lead_weight, tail_weight, shifts, exponent):
    pole_count = pole_sq.shape[0]
    step_len = min(4096, pole_count)
    blocks = pole_count // step_len

    def visit_block(running, block_items):
        sq_block, lead_block, tail_block = block_items
        inverse = 1.0 / (sq_block[:, None] - shifts[None, :])
        leading = inverse if exponent == 1 else inverse * inverse
        return ((running[0] + lax.optimization_barrier(jnp.sum(lead_block[:, None] * leading, 0)), running[1] + lax.optimization_barrier(jnp.sum(tail_block[:, None] * inverse * inverse, 0))), None)
    initial = (jnp.zeros(shifts.shape, jnp.float32), jnp.zeros(shifts.shape, jnp.float32))
    block_items = (pole_sq.reshape(blocks, step_len), lead_weight.reshape(blocks, step_len), tail_weight.reshape(blocks, step_len))
    totals, _ = lax.scan(visit_block, initial, block_items)
    return totals

def apply_blocks(vectors, placed, block_flags):
    stacked = vectors.reshape(ROW_BLOCKS, R_DEV, KH)

    def one_block(pair):
        keep_mask = jnp.repeat(pair[1], BW).astype(jnp.bfloat16)
        return jnp.dot(pair[0], placed * keep_mask[:, None], preferred_element_type=jnp.float32)
    result = lax.map(one_block, (stacked, block_flags))
    return result.reshape(ROWS, NR).astype(jnp.bfloat16)

def reference(poles, coupling, kinds, permutation, block_map, left_vectors, right_vectors):
    total_poles = poles.shape[0]
    half_poles = total_poles // 2
    pole_sq = poles * poles
    alive = (kinds != 0).astype(jnp.float32)
    in_left = ((kinds == 1) | (kinds == 2)).astype(jnp.float32)
    in_right = ((kinds == 2) | (kinds == 3)).astype(jnp.float32)
    weight = alive * coupling * coupling
    u_weight = in_left * coupling * coupling
    v_weight = in_right * pole_sq * coupling * coupling
    coef_u = in_left * coupling
    coef_v = in_right * poles * coupling
    ranks = jnp.arange(P_SIZE, dtype=jnp.int32)
    root_index = jnp.concatenate([half_poles - P_SIZE + ranks, total_poles - 2 * P_SIZE + ranks]).astype(jnp.int32)
    lower_pole = pole_sq[root_index]
    upper_pole = pole_sq[root_index + 1]
    pole_gap = upper_pole - lower_pole
    low_bound = lower_pole + 0.1 * pole_gap
    high_bound = upper_pole - 0.1 * pole_gap
    shifts = lower_pole + 0.5 * pole_gap
    for step in range(ITERS):
        sum_value, slope_value = inverse_sums(pole_sq, weight, weight, shifts, 1)
        secular_value = 1.0 + sum_value
        shifts = jnp.clip(shifts - 0.5 * secular_value / slope_value, low_bound, high_bound)
    root_offsets = (shifts - lower_pole) / pole_gap
    sum_u, sum_v = inverse_sums(pole_sq, u_weight, v_weight, shifts, 2)
    norm_u = jnp.sqrt(sum_u)
    norm_v = jnp.sqrt(1.0 + sum_v)
    outs_left = []
    outs_right = []
    for side_id in range(2):
        begin = side_id * half_poles
        child_sq = pole_sq[begin:begin + half_poles]
        inverse = 1.0 / (child_sq[:, None] - shifts[None, :])
        rows_u = (coef_u[begin:begin + half_poles][:, None] * inverse / norm_u[None, :]).astype(jnp.bfloat16)
        rows_v = (coef_v[begin:begin + half_poles][:, None] * inverse / norm_v[None, :]).astype(jnp.bfloat16)
        placing = permutation[side_id]
        placed_u = jnp.zeros((half_poles, NR), jnp.bfloat16).at[placing].set(rows_u)
        placed_v = jnp.zeros((half_poles, NR), jnp.bfloat16).at[placing].set(rows_v)
        outs_left.append(apply_blocks(left_vectors[side_id], placed_u, block_map[side_id, :, 0]))
        outs_right.append(apply_blocks(right_vectors[side_id], placed_v, block_map[side_id, :, 1]))
    return (jnp.stack(outs_left), jnp.stack(outs_right), root_offsets)
```

```python
import functools

import jax
import jax.numpy as jnp
from jax import lax
from jax.experimental import pallas as pl
from jax.experimental.pallas import tpu as pltpu
from jax.sharding import PartitionSpec as P

MESH = pl.DeviceIdType.MESH
ITERS = 8
LANES = 128
BW = 256
CHUNK = 4096
F32 = jnp.float32
BF16 = jnp.bfloat16


def far_first(i):
    return (2 + i + i // 2 + 2 * (i // 3)) % 4


def chip_at(grp, i):
    x = (grp // 16 + far_first(i // 16)) % 4
    y = (grp // 4 + far_first((i // 4) % 4)) % 4
    z = (grp + far_first(i % 4)) % 4
    return x * 16 + y * 4 + z


def recip(value):
    guess = pl.reciprocal(value, approx=True)
    return guess + guess * (1.0 - value * guess)


def total(value):
    return jnp.sum(value, axis=(0, 1), keepdims=True)


def merge_kernel(
    poles_ref, coupling_ref, kinds_ref, perm_ref, map_ref, left_ref, right_ref,
    out_left, out_right, out_offsets,
    held, raw, one_hot, pieces, spread, found, placed, sq, weight, answers,
    shift_cols, cauchy_a, cauchy_b, acc, load_sem, send_sem, recv_sem,
):
    side = lax.axis_index("side")
    grp = lax.axis_index("grp")
    me = side * 64 + grp
    rows = left_ref.shape[0]
    count = left_ref.shape[1]
    groups = raw.shape[1]

    loads = [
        pltpu.make_async_copy(left_ref, held.at[pl.ds(0, rows)], load_sem.at[0]),
        pltpu.make_async_copy(right_ref, held.at[pl.ds(rows, rows)], load_sem.at[1]),
    ]
    for load in loads:
        load.start()

    barrier = pltpu.get_barrier_semaphore()

    def greet(i, _):
        other = (me + 1 + i) % 128
        pl.semaphore_signal(barrier, inc=1, device_id=(other // 64, other % 64), device_id_type=MESH)
        return 0

    lax.fori_loop(0, 127, greet, 0)

    raw[side, grp, 0] = poles_ref[...]
    raw[side, grp, 1] = coupling_ref[...]
    raw[side, grp, 2] = kinds_ref[...].astype(F32)
    low_digit = lax.broadcasted_iota(jnp.int32, (LANES, LANES), 0)

    def mark(r, _):
        own = perm_ref[pl.ds(r, 1), :] % LANES
        columns = pl.ds(pl.multiple_of(r * LANES, LANES), LANES)
        one_hot[:, columns] = jnp.where(own == low_digit, 1.0, 0.0).astype(BF16)
        return 0

    lax.fori_loop(0, count // LANES, mark, 0, unroll=4)

    pl.semaphore_wait(barrier, 127)

    def send_raw(i, _):
        mine = raw.at[side, grp]
        pltpu.make_async_remote_copy(
            src_ref=mine, dst_ref=mine, send_sem=send_sem.at[0], recv_sem=recv_sem.at[0],
            device_id=(side, chip_at(grp, i)), device_id_type=MESH,
        ).start()
        return 0

    lax.fori_loop(0, 63, send_raw, 0)
    gathered = pltpu.make_async_remote_copy(
        src_ref=raw.at[0, pl.ds(0, 63)], dst_ref=raw.at[0, pl.ds(0, 63)], send_sem=send_sem.at[0],
        recv_sem=recv_sem.at[0], device_id=(1 - side, grp), device_id_type=MESH,
    )
    gathered.wait_recv()

    cross = pltpu.make_async_remote_copy(
        src_ref=raw.at[side], dst_ref=raw.at[side], send_sem=send_sem.at[1], recv_sem=recv_sem.at[1],
        device_id=(1 - side, grp), device_id_type=MESH,
    )
    cross.start()

    def split(j, _):
        pole = raw[side, j, 0]
        coupling = raw[side, j, 1]
        kind = raw[side, j, 2]
        coef_u = jnp.where((kind == 1.0) | (kind == 2.0), coupling, 0.0)
        coef_v = jnp.where(kind >= 2.0, pole * coupling, 0.0)
        square = pole * pole
        high = square.astype(BF16).astype(F32)
        rest = square - high
        middle = rest.astype(BF16).astype(F32)
        u_high = coef_u.astype(BF16).astype(F32)
        v_high = coef_v.astype(BF16).astype(F32)
        for q, piece in enumerate((high, middle, rest - middle, u_high, coef_u - u_high, v_high, coef_v - v_high)):
            pieces[pl.ds(j * 4, 4), q, :] = piece
        return 0

    pieces[:, 7, :] = jnp.zeros_like(pieces[:, 7, :])
    lax.fori_loop(0, groups, split, 0, unroll=2)

    def mask(r, _):
        digit = perm_ref[pl.ds(r, 1), :] // LANES - 4 * grp
        piece = pieces[r]
        columns = pl.ds(pl.multiple_of(r * LANES, LANES), LANES)
        spread[:, columns] = jnp.concatenate(
            [jnp.where(digit == h, piece, 0.0) for h in range(4)], axis=0
        ).astype(BF16)
        return 0

    lax.fori_loop(0, count // LANES, mask, 0, unroll=4)
    found[...] = jnp.zeros_like(found)

    def look_up(i, _):
        columns = pl.ds(pl.multiple_of(i * CHUNK, CHUNK), CHUNK)
        found[...] += lax.dot_general(
            spread[:, columns], one_hot[:, columns], (((1,), (1,)), ((), ())), preferred_element_type=F32
        )
        return 0

    lax.fori_loop(0, count // CHUNK, look_up, 0)
    digits = [found[pl.ds(q, 4, stride=8), :] for q in range(7)]
    placed[grp, 0] = digits[0] + (digits[1] + digits[2])
    placed[grp, 1] = digits[3] + digits[4]
    placed[grp, 2] = digits[5] + digits[6]

    def send_placed(i, _):
        mine = placed.at[grp]
        pltpu.make_async_remote_copy(
            src_ref=mine, dst_ref=mine, send_sem=send_sem.at[2], recv_sem=recv_sem.at[2],
            device_id=(side, chip_at(grp, i)), device_id_type=MESH,
        ).start()
        return 0

    lax.fori_loop(0, 63, send_placed, 0)

    cross.wait_recv()

    def lay_out(j, _):
        pole = jnp.concatenate([raw[0, j, 0], raw[1, j, 0]], axis=0)
        coupling = jnp.concatenate([raw[0, j, 1], raw[1, j, 1]], axis=0)
        kind = jnp.concatenate([raw[0, j, 2], raw[1, j, 2]], axis=0)
        sq[j] = pole * pole
        weight[j] = jnp.where(kind != 0.0, coupling, 0.0) * coupling
        return 0

    lax.fori_loop(0, groups, lay_out, 0, unroll=4)

    lane = lax.broadcasted_iota(jnp.int32, (1, LANES), 1)
    last = groups - 1

    def pick(row, at):
        return total(jnp.where(lane == at, row, 0.0))

    after = jnp.where(me == 127, 0, -1)
    first_low = pick(sq[last, 3:4], me)
    first_high = pick(sq[last, 3:4], me + 1) + pick(sq[0, 4:5], after)
    second_low = pick(sq[last, 6:7], me)
    second_high = pick(sq[last, 6:7], me + 1) + pick(sq[last, 7:8], after)
    lows = (first_low, second_low)
    gaps = (first_high - first_low, second_high - second_low)
    starts = tuple(low + 0.1 * gap for low, gap in zip(lows, gaps))
    ends = tuple(high - 0.1 * gap for high, gap in zip((first_high, second_high), gaps))
    blocks = 8

    def visit(shifts, extra):
        zero = jnp.zeros((8, LANES), F32)
        sums = [[zero, zero], [zero, zero]]
        wide = [jnp.broadcast_to(shift, (8, LANES)) for shift in shifts]
        for b in range(groups // blocks):
            at = pl.ds(b * blocks, blocks)
            sq_block = sq[at]
            lead, tail = extra(at, sq_block)
            for k in range(2):
                inverse = recip(sq_block - wide[k])
                if lead is None:
                    part = tail * inverse
                    sums[k][0] = sums[k][0] + jnp.sum(part, axis=0)
                    sums[k][1] = sums[k][1] + jnp.sum(part * inverse, axis=0)
                else:
                    squared = inverse * inverse
                    sums[k][0] = sums[k][0] + jnp.sum(lead * squared, axis=0)
                    sums[k][1] = sums[k][1] + jnp.sum(tail * squared, axis=0)
        return [[total(s) for s in pair] for pair in sums]

    def step(_, shifts):
        sums = visit(shifts, lambda at, sq_block: (None, weight[at]))
        return tuple(
            jnp.clip(shift - 0.5 * (1.0 + value) / slope, start, end)
            for shift, (value, slope), start, end in zip(shifts, sums, starts, ends)
        )

    shifts = lax.fori_loop(
        0, ITERS, step, tuple(low + 0.5 * gap for low, gap in zip(lows, gaps))
    )

    def norm_weights(at, sq_block):
        kind = jnp.concatenate([raw[0, at, 2], raw[1, at, 2]], axis=1)
        both = weight[at]
        return (
            jnp.where((kind == 1.0) | (kind == 2.0), both, 0.0),
            jnp.where(kind >= 2.0, sq_block * both, 0.0),
        )

    norms = visit(shifts, norm_weights)
    values = [shifts[0], shifts[1]]
    values += [lax.rsqrt(norms[k][0]) for k in range(2)]
    values += [lax.rsqrt(1.0 + norms[k][1]) for k in range(2)]
    values += [(shift - low) / gap for shift, low, gap in zip(shifts, lows, gaps)]
    row = jnp.zeros((1, LANES), F32)
    for k, value in enumerate(values):
        row = jnp.where(lane == k, value, row)
    answers[me] = row

    def send_answer(i, _):
        mine = answers.at[me]
        pltpu.make_async_remote_copy(
            src_ref=mine, dst_ref=mine, send_sem=send_sem.at[3], recv_sem=recv_sem.at[3],
            device_id=((side + i) % 2, chip_at(grp, i // 2)), device_id_type=MESH,
        ).start()
        return 0

    lax.fori_loop(0, 126, send_answer, 0)
    mine = answers.at[me]
    pltpu.make_async_remote_copy(
        src_ref=mine, dst_ref=mine, send_sem=send_sem.at[3], recv_sem=recv_sem.at[3],
        device_id=(1 - side, grp), device_id_type=MESH,
    ).start()

    for load in loads:
        load.wait()
    placing = pltpu.make_async_remote_copy(
        src_ref=placed.at[pl.ds(0, 63)], dst_ref=placed.at[pl.ds(0, 63)], send_sem=send_sem.at[2],
        recv_sem=recv_sem.at[2], device_id=(1 - side, grp), device_id_type=MESH,
    )
    placing.wait_recv()

    def scale(j, _):
        for h in range(4):
            columns = pl.ds(pl.multiple_of(j * 512 + h * LANES, LANES), LANES)
            for m in range(2):
                coef = placed[j, 1 + m, h:h + 1, :]
                keep = map_ref[m, j * 2 + h // 2]
                coef = jnp.where(keep != 0, coef, 0.0)
                part = pl.ds(m * rows, rows)
                held[part, columns] = held[part, columns] * jnp.broadcast_to(coef, (rows, LANES)).astype(BF16)
        return 0

    lax.fori_loop(0, groups, scale, 0)
    acc[...] = jnp.zeros_like(acc)

    answered = pltpu.make_async_remote_copy(
        src_ref=answers.at[pl.ds(0, 127)], dst_ref=answers.at[pl.ds(0, 127)], send_sem=send_sem.at[3],
        recv_sem=recv_sem.at[3], device_id=(1 - side, grp), device_id_type=MESH,
    )
    answered.wait_recv()

    table = answers[:, 0, :]
    shift_cols[pl.ds(0, LANES)] = jnp.broadcast_to(table[:, 0:1], (LANES, LANES))
    shift_cols[pl.ds(LANES, LANES)] = jnp.broadcast_to(table[:, 1:2], (LANES, LANES))

    def fill(i, cauchy):
        shift = shift_cols[...]
        for j in range(CHUNK // 512):
            for h in range(4):
                difference = placed[i * (CHUNK // 512) + j, 0, h:h + 1, :] - shift
                cauchy[:, pl.ds(j * 512 + h * LANES, LANES)] = pl.reciprocal(difference, approx=True).astype(BF16)

    def multiply(i, cauchy):
        columns = pl.ds(pl.multiple_of(i * CHUNK, CHUNK), CHUNK)
        acc[...] += lax.dot_general(
            held[:, columns], cauchy[...], (((1,), (1,)), ((), ())), preferred_element_type=F32
        )

    chunks = count // CHUNK
    fill(0, cauchy_a)

    def pair(i, _):
        fill(2 * i + 1, cauchy_b)
        multiply(2 * i, cauchy_a)
        fill((2 * i + 2) % chunks, cauchy_a)
        multiply(2 * i + 1, cauchy_b)
        return 0

    lax.fori_loop(0, chunks // 2, pair, 0)
    turned = table.T
    norm_u = jnp.concatenate([turned[2:3], turned[3:4]], axis=1)
    norm_v = jnp.concatenate([turned[4:5], turned[5:6]], axis=1)
    out_left[...] = (acc[pl.ds(0, rows)] * norm_u).astype(BF16)
    out_right[...] = (acc[pl.ds(rows, rows)] * norm_v).astype(BF16)
    out_offsets[...] = turned[6:8]
    gathered.wait_send()
    cross.wait_send()
    placing.wait_send()
    answered.wait_send()


def on_device(poles, coupling, kinds, permutation, block_map, left_vectors, right_vectors):
    rows, count = left_vectors.shape[1:]
    own = poles.shape[0] // LANES
    groups = lax.axis_size("grp")
    vmem = pl.BlockSpec(memory_space=pltpu.VMEM)
    anywhere = pl.BlockSpec(memory_space=pl.ANY)
    left, right, offsets = pl.pallas_call(
        merge_kernel,
        out_shape=(
            jax.ShapeDtypeStruct((rows, 2 * LANES), BF16),
            jax.ShapeDtypeStruct((rows, 2 * LANES), BF16),
            jax.ShapeDtypeStruct((2, LANES), F32),
        ),
        in_specs=[vmem, vmem, vmem, vmem, pl.BlockSpec(memory_space=pltpu.SMEM), anywhere, anywhere],
        out_specs=(vmem, vmem, vmem),
        scratch_shapes=[
            pltpu.VMEM((2 * rows, count), BF16),
            pltpu.VMEM((2, groups, 3, own, LANES), F32),
            pltpu.VMEM((LANES, count), BF16),
            pltpu.VMEM((count // LANES, 8, LANES), F32),
            pltpu.VMEM((32, count), BF16),
            pltpu.VMEM((32, LANES), F32),
            pltpu.VMEM((groups, 3, own, LANES), F32),
            pltpu.VMEM((groups, 8, LANES), F32),
            pltpu.VMEM((groups, 8, LANES), F32),
            pltpu.VMEM((2 * groups, 1, LANES), F32),
            pltpu.VMEM((2 * LANES, LANES), F32),
            pltpu.VMEM((2 * LANES, CHUNK), BF16),
            pltpu.VMEM((2 * LANES, CHUNK), BF16),
            pltpu.VMEM((2 * rows, 2 * LANES), F32),
            pltpu.SemaphoreType.DMA((2,)),
            pltpu.SemaphoreType.DMA((4,)),
            pltpu.SemaphoreType.DMA((4,)),
        ],
        compiler_params=pltpu.CompilerParams(
            collective_id=0, has_side_effects=True, vmem_limit_bytes=58 * 2**20
        ),
    )(
        poles.reshape(own, LANES),
        coupling.reshape(own, LANES),
        kinds.reshape(own, LANES),
        permutation.reshape(count // LANES, LANES),
        block_map[0, 0],
        left_vectors[0],
        right_vectors[0],
    )
    return left[None], right[None], offsets.reshape(2 * LANES)


def solution(mesh):
    return jax.shard_map(
        on_device,
        mesh=mesh,
        in_specs=(
            P(("side", "grp")),
            P(("side", "grp")),
            P(("side", "grp")),
            P("side", None),
            P("side", "grp", None, None),
            P("side", "grp", None),
            P("side", "grp", None),
        ),
        out_specs=(P("side", "grp", None), P("side", "grp", None), P()),
        check_vma=False,
    )
```

```python
import functools

import jax
import jax.numpy as jnp
from jax import lax
from jax.experimental import pallas as pl
from jax.experimental.pallas import tpu as pltpu
from jax.sharding import PartitionSpec as P

MESH = pl.DeviceIdType.MESH
ITERS = 8
LANES = 128
BW = 256
LOW = 64
CHUNK = 4096
STRIP = 1024
F32 = jnp.float32
BF16 = jnp.bfloat16


def visit_chips(grp, act):
    far_first = (2, 3, 1, 0)
    x, rest = lax.div(grp, 16), lax.rem(grp, 16)
    y, z = lax.div(rest, 4), lax.rem(rest, 4)
    xs = [16 * lax.rem(x + far, 4) for far in far_first]
    ys = [4 * lax.rem(y + far, 4) for far in far_first]
    zs = [lax.rem(z + far, 4) for far in far_first]
    for i in range(63):
        act(xs[i // 16] + ys[i // 4 % 4] + zs[i % 4])


def recip(value):
    guess = pl.reciprocal(value, approx=True)
    return guess + guess * (1.0 - value * guess)


def total(value):
    return jnp.sum(value, axis=(0, 1), keepdims=True)


def merge_kernel(
    poles_ref, coupling_ref, kinds_ref, perm_ref, map_ref, left_ref, right_ref,
    out_left, out_right, out_offsets,
    held, raw, one_hot, pieces, spread, found, placed, sq, weight, answers,
    shift_cols, coefs, cauchy_a, cauchy_b, acc, load_sem, send_sem, recv_sem,
):
    side = lax.axis_index("side")
    grp = lax.axis_index("grp")
    me = side * 64 + grp
    rows = left_ref.shape[0]
    count = left_ref.shape[1]
    groups = raw.shape[1]

    loads = [
        pltpu.make_async_copy(left_ref, held.at[pl.ds(0, rows)], load_sem.at[0]),
        pltpu.make_async_copy(right_ref, held.at[pl.ds(rows, rows)], load_sem.at[1]),
    ]
    for load in loads:
        load.start()

    barrier = pltpu.get_barrier_semaphore()

    def greet(chip, core):
        pl.semaphore_signal(barrier, inc=1, device_id=(core, chip), device_id_type=MESH)

    visit_chips(grp, lambda chip: greet(chip, side))
    greet(grp, 1 - side)

    raw[side, grp, 0] = poles_ref[...]
    raw[side, grp, 1] = coupling_ref[...]
    raw[side, grp, 2] = kinds_ref[...].astype(F32)
    low_digit = lax.broadcasted_iota(jnp.int32, (LOW, LANES), 0)

    def mark(r, _):
        own = perm_ref[pl.ds(r, 1), :] % LOW
        columns = pl.ds(pl.multiple_of(r * LANES, LANES), LANES)
        one_hot[:, columns] = jnp.where(own == low_digit, 1.0, 0.0).astype(BF16)
        return 0

    lax.fori_loop(0, count // LANES, mark, 0, unroll=4)

    pl.semaphore_wait(barrier, 64)

    def send(mine, k, chip, core):
        pltpu.make_async_remote_copy(
            src_ref=mine, dst_ref=mine, send_sem=send_sem.at[k], recv_sem=recv_sem.at[k],
            device_id=(core, chip), device_id_type=MESH,
        ).start()

    visit_chips(grp, lambda chip: send(raw.at[side, grp], 0, chip, side))
    gathered = pltpu.make_async_remote_copy(
        src_ref=raw.at[0, pl.ds(0, 63)], dst_ref=raw.at[0, pl.ds(0, 63)], send_sem=send_sem.at[0],
        recv_sem=recv_sem.at[0], device_id=(1 - side, grp), device_id_type=MESH,
    )
    gathered.wait_recv()

    cross = pltpu.make_async_remote_copy(
        src_ref=raw.at[side], dst_ref=raw.at[side], send_sem=send_sem.at[1], recv_sem=recv_sem.at[1],
        device_id=(1 - side, grp), device_id_type=MESH,
    )
    cross.start()

    def split(j, _):
        pole = raw[side, j, 0]
        coupling = raw[side, j, 1]
        kind = raw[side, j, 2]
        coef_u = jnp.where((kind == 1.0) | (kind == 2.0), coupling, 0.0)
        coef_v = jnp.where(kind >= 2.0, pole * coupling, 0.0)
        square = pole * pole
        high = square.astype(BF16).astype(F32)
        rest = square - high
        middle = rest.astype(BF16).astype(F32)
        u_high = coef_u.astype(BF16).astype(F32)
        v_high = coef_v.astype(BF16).astype(F32)
        for q, piece in enumerate((high, middle, rest - middle, u_high, coef_u - u_high, v_high, coef_v - v_high)):
            pieces[pl.ds(j * 4, 4), q, :] = piece
        return 0

    pieces[:, 7, :] = jnp.zeros_like(pieces[:, 7, :])
    lax.fori_loop(0, groups, split, 0, unroll=2)

    def mask(r, _):
        digit = perm_ref[pl.ds(r, 1), :] // LOW - 8 * grp
        piece = pieces[r]
        columns = pl.ds(pl.multiple_of(r * LANES, LANES), LANES)
        spread[:, columns] = jnp.concatenate(
            [jnp.where(digit == h, piece, 0.0) for h in range(8)], axis=0
        ).astype(BF16)
        return 0

    lax.fori_loop(0, count // LANES, mask, 0, unroll=4)
    found[...] = jnp.zeros_like(found)

    def look_up(i, _):
        columns = pl.ds(pl.multiple_of(i * CHUNK, CHUNK), CHUNK)
        found[...] += lax.dot_general(
            spread[:, columns], one_hot[:, columns], (((1,), (1,)), ((), ())), preferred_element_type=F32
        )
        return 0

    lax.fori_loop(0, count // CHUNK, look_up, 0)
    digits = [
        jnp.concatenate([found[pl.ds(q + 8 * half, 4, stride=16), :] for half in range(2)], axis=1)
        for q in range(7)
    ]
    placed[grp, 0] = digits[0] + (digits[1] + digits[2])
    placed[grp, 1] = digits[3] + digits[4]
    placed[grp, 2] = digits[5] + digits[6]

    visit_chips(grp, lambda chip: send(placed.at[grp], 2, chip, side))

    cross.wait_recv()

    def lay_out(j, _):
        pole = jnp.concatenate([raw[0, j, 0], raw[1, j, 0]], axis=0)
        coupling = jnp.concatenate([raw[0, j, 1], raw[1, j, 1]], axis=0)
        kind = jnp.concatenate([raw[0, j, 2], raw[1, j, 2]], axis=0)
        sq[j] = pole * pole
        weight[j] = jnp.where(kind != 0.0, coupling, 0.0) * coupling
        return 0

    lax.fori_loop(0, groups, lay_out, 0, unroll=4)

    lane = lax.broadcasted_iota(jnp.int32, (1, LANES), 1)
    last = groups - 1

    def pick(row, at):
        return total(jnp.where(lane == at, row, 0.0))

    after = jnp.where(me == 127, 0, -1)
    first_low = pick(sq[last, 3:4], me)
    first_high = pick(sq[last, 3:4], me + 1) + pick(sq[0, 4:5], after)
    second_low = pick(sq[last, 6:7], me)
    second_high = pick(sq[last, 6:7], me + 1) + pick(sq[last, 7:8], after)
    lows = (first_low, second_low)
    gaps = (first_high - first_low, second_high - second_low)
    starts = tuple(low + 0.1 * gap for low, gap in zip(lows, gaps))
    ends = tuple(high - 0.1 * gap for high, gap in zip((first_high, second_high), gaps))
    blocks = 8

    def visit(shifts, extra):
        zero = jnp.zeros((8, LANES), F32)
        sums = [[zero, zero], [zero, zero]]
        wide = [jnp.broadcast_to(shift, (8, LANES)) for shift in shifts]
        for b in range(groups // blocks):
            at = pl.ds(b * blocks, blocks)
            sq_block = sq[at]
            lead, tail = extra(at, sq_block)
            for k in range(2):
                inverse = recip(sq_block - wide[k])
                if lead is None:
                    part = tail * inverse
                    sums[k][0] = sums[k][0] + jnp.sum(part, axis=0)
                    sums[k][1] = sums[k][1] + jnp.sum(part * inverse, axis=0)
                else:
                    squared = inverse * inverse
                    sums[k][0] = sums[k][0] + jnp.sum(lead * squared, axis=0)
                    sums[k][1] = sums[k][1] + jnp.sum(tail * squared, axis=0)
        return [[total(s) for s in pair] for pair in sums]

    def step(_, shifts):
        sums = visit(shifts, lambda at, sq_block: (None, weight[at]))
        return tuple(
            jnp.clip(shift - 0.5 * (1.0 + value) / slope, start, end)
            for shift, (value, slope), start, end in zip(shifts, sums, starts, ends)
        )

    shifts = lax.fori_loop(
        0, ITERS, step, tuple(low + 0.5 * gap for low, gap in zip(lows, gaps))
    )

    def norm_weights(at, sq_block):
        kind = jnp.concatenate([raw[0, at, 2], raw[1, at, 2]], axis=1)
        both = weight[at]
        return (
            jnp.where((kind == 1.0) | (kind == 2.0), both, 0.0),
            jnp.where(kind >= 2.0, sq_block * both, 0.0),
        )

    norms = visit(shifts, norm_weights)
    values = [shifts[0], shifts[1]]
    values += [lax.rsqrt(norms[k][0]) for k in range(2)]
    values += [lax.rsqrt(1.0 + norms[k][1]) for k in range(2)]
    values += [(shift - low) / gap for shift, low, gap in zip(shifts, lows, gaps)]
    row = jnp.zeros((1, LANES), F32)
    for k, value in enumerate(values):
        row = jnp.where(lane == k, value, row)
    answers[me] = row

    def send_answer(chip):
        for core in (side, 1 - side):
            send(answers.at[me], 3, chip, core)

    visit_chips(grp, send_answer)
    send(answers.at[me], 3, grp, 1 - side)

    for load in loads:
        load.wait()
    placing = pltpu.make_async_remote_copy(
        src_ref=placed.at[pl.ds(0, 63)], dst_ref=placed.at[pl.ds(0, 63)], send_sem=send_sem.at[2],
        recv_sem=recv_sem.at[2], device_id=(1 - side, grp), device_id_type=MESH,
    )
    placing.wait_recv()

    def spread_coefs(j, _):
        for h in range(4):
            columns = pl.ds(pl.multiple_of(j * 512 + h * LANES, LANES), LANES)
            for m in range(2):
                coef = jnp.where(map_ref[m, j * 2 + h // 2] != 0, placed[j, 1 + m, h:h + 1, :], 0.0)
                coefs[m, :, columns] = jnp.broadcast_to(coef, (16, LANES)).astype(BF16)
        return 0

    lax.fori_loop(0, groups, spread_coefs, 0)

    def scale(i, _):
        columns = pl.ds(pl.multiple_of(i * STRIP, STRIP), STRIP)
        for m in range(2):
            coef = coefs[m, :, columns]
            for t in range(rows // 16):
                part = pl.ds(m * rows + t * 16, 16)
                held[part, columns] = held[part, columns] * coef
        return 0

    lax.fori_loop(0, count // STRIP, scale, 0)
    acc[...] = jnp.zeros_like(acc)

    answered = pltpu.make_async_remote_copy(
        src_ref=answers.at[pl.ds(0, 127)], dst_ref=answers.at[pl.ds(0, 127)], send_sem=send_sem.at[3],
        recv_sem=recv_sem.at[3], device_id=(1 - side, grp), device_id_type=MESH,
    )
    answered.wait_recv()

    table = answers[:, 0, :]
    shift_cols[pl.ds(0, LANES)] = jnp.broadcast_to(table[:, 0:1], (LANES, LANES))
    shift_cols[pl.ds(LANES, LANES)] = jnp.broadcast_to(table[:, 1:2], (LANES, LANES))

    def fill(i, cauchy):
        shift = shift_cols[...]
        for j in range(CHUNK // 512):
            for h in range(4):
                difference = placed[i * (CHUNK // 512) + j, 0, h:h + 1, :] - shift
                cauchy[:, pl.ds(j * 512 + h * LANES, LANES)] = pl.reciprocal(difference, approx=True).astype(BF16)

    def multiply(i, cauchy):
        columns = pl.ds(pl.multiple_of(i * CHUNK, CHUNK), CHUNK)
        acc[...] += lax.dot_general(
            held[:, columns], cauchy[...], (((1,), (1,)), ((), ())), preferred_element_type=F32
        )

    chunks = count // CHUNK
    fill(0, cauchy_a)

    def pair(i, _):
        fill(2 * i + 1, cauchy_b)
        multiply(2 * i, cauchy_a)
        fill((2 * i + 2) % chunks, cauchy_a)
        multiply(2 * i + 1, cauchy_b)
        return 0

    lax.fori_loop(0, chunks // 2, pair, 0)
    turned = table.T
    norm_u = jnp.concatenate([turned[2:3], turned[3:4]], axis=1)
    norm_v = jnp.concatenate([turned[4:5], turned[5:6]], axis=1)
    out_left[...] = (acc[pl.ds(0, rows)] * norm_u).astype(BF16)
    out_right[...] = (acc[pl.ds(rows, rows)] * norm_v).astype(BF16)
    out_offsets[...] = turned[6:8]
    gathered.wait_send()
    cross.wait_send()
    placing.wait_send()
    answered.wait_send()


def hand_over(left_ref, right_ref, offsets_ref, out_left, out_right, out_offsets):
    out_left[...] = left_ref[...]
    out_right[...] = right_ref[...]
    out_offsets[...] = offsets_ref[...]


def on_device(poles, coupling, kinds, permutation, block_map, left_vectors, right_vectors):
    rows, count = left_vectors.shape[1:]
    own = poles.shape[0] // LANES
    groups = lax.axis_size("grp")
    vmem = pl.BlockSpec(memory_space=pltpu.VMEM)
    anywhere = pl.BlockSpec(memory_space=pl.ANY)
    left, right, offsets = pl.pallas_call(
        merge_kernel,
        out_shape=(
            jax.ShapeDtypeStruct((rows, 2 * LANES), BF16),
            jax.ShapeDtypeStruct((rows, 2 * LANES), BF16),
            jax.ShapeDtypeStruct((2, LANES), F32),
        ),
        in_specs=[vmem, vmem, vmem, vmem, pl.BlockSpec(memory_space=pltpu.SMEM), anywhere, anywhere],
        out_specs=(vmem, vmem, vmem),
        scratch_shapes=[
            pltpu.VMEM((2 * rows, count), BF16),
            pltpu.VMEM((2, groups, 3, own, LANES), F32),
            pltpu.VMEM((LOW, count), BF16),
            pltpu.VMEM((count // LANES, 8, LANES), F32),
            pltpu.VMEM((64, count), BF16),
            pltpu.VMEM((64, LOW), F32),
            pltpu.VMEM((groups, 3, own, LANES), F32),
            pltpu.VMEM((groups, 8, LANES), F32),
            pltpu.VMEM((groups, 8, LANES), F32),
            pltpu.VMEM((2 * groups, 1, LANES), F32),
            pltpu.VMEM((2 * LANES, LANES), F32),
            pltpu.VMEM((2, 16, count), BF16),
            pltpu.VMEM((2 * LANES, CHUNK), BF16),
            pltpu.VMEM((2 * LANES, CHUNK), BF16),
            pltpu.VMEM((2 * rows, 2 * LANES), F32),
            pltpu.SemaphoreType.DMA((2,)),
            pltpu.SemaphoreType.DMA((4,)),
            pltpu.SemaphoreType.DMA((4,)),
        ],
        compiler_params=pltpu.CompilerParams(
            collective_id=0, has_side_effects=True, vmem_limit_bytes=58 * 2**20
        ),
    )(
        poles.reshape(own, LANES),
        coupling.reshape(own, LANES),
        kinds.reshape(own, LANES),
        permutation.reshape(count // LANES, LANES),
        block_map[0, 0],
        left_vectors[0],
        right_vectors[0],
    )
    left, right, offsets = pl.pallas_call(
        hand_over,
        out_shape=(
            jax.ShapeDtypeStruct(left.shape, BF16),
            jax.ShapeDtypeStruct(right.shape, BF16),
            jax.ShapeDtypeStruct(offsets.shape, F32),
        ),
        in_specs=[vmem] * 3,
        out_specs=(vmem,) * 3,
    )(left, right, offsets)
    return left[None], right[None], offsets.reshape(2 * LANES)


def solution(mesh):
    return jax.shard_map(
        on_device,
        mesh=mesh,
        in_specs=(
            P(("side", "grp")),
            P(("side", "grp")),
            P(("side", "grp")),
            P("side", None),
            P("side", "grp", None, None),
            P("side", "grp", None),
            P("side", "grp", None),
        ),
        out_specs=(P("side", "grp", None), P("side", "grp", None), P()),
        check_vma=False,
    )
```

```python
import functools

import jax
import jax.numpy as jnp
from jax import lax
from jax.experimental import pallas as pl
from jax.experimental.pallas import tpu as pltpu
from jax.sharding import PartitionSpec as P

MESH = pl.DeviceIdType.MESH
ITERS = 8
LANES = 128
BW = 256
LOW = 64
CHUNK = 4096
STRIP = 1024
F32 = jnp.float32
BF16 = jnp.bfloat16


def visit_chips(grp, act):
    far_first = (2, 3, 1, 0)
    x, rest = lax.div(grp, 16), lax.rem(grp, 16)
    y, z = lax.div(rest, 4), lax.rem(rest, 4)
    xs = [16 * lax.rem(x + far, 4) for far in far_first]
    ys = [4 * lax.rem(y + far, 4) for far in far_first]
    zs = [lax.rem(z + far, 4) for far in far_first]
    for i in range(63):
        act(xs[i // 16] + ys[i // 4 % 4] + zs[i % 4])


def recip(value):
    guess = pl.reciprocal(value, approx=True)
    return guess + guess * (1.0 - value * guess)


def total(value):
    return jnp.sum(value, axis=(0, 1), keepdims=True)


def merge_kernel(
    poles_ref, coupling_ref, kinds_hbm, perm_hbm, map_hbm, left_ref, right_ref,
    out_left, out_right, out_offsets,
    perm_ref, kinds_ref, map_ref, held, raw, one_hot, pieces, spread, found, placed, sq, weight, answers,
    shift_cols, coefs, cauchy_a, cauchy_b, acc, load_sem, send_sem, recv_sem,
):
    side = lax.axis_index("side")
    grp = lax.axis_index("grp")
    me = side * 64 + grp
    rows = left_ref.shape[0]
    count = left_ref.shape[1]
    groups = raw.shape[1]

    barrier = pltpu.get_barrier_semaphore()

    def greet(chip, core):
        pl.semaphore_signal(barrier, inc=1, device_id=(core, chip), device_id_type=MESH)

    visit_chips(grp, lambda chip: greet(chip, side))
    greet(grp, 1 - side)

    small = [
        pltpu.make_async_copy(source, target, load_sem.at[2 + k])
        for k, (source, target) in enumerate((
            (perm_hbm, perm_ref), (poles_ref, raw.at[side, grp, 0]), (coupling_ref, raw.at[side, grp, 1]),
            (kinds_hbm, kinds_ref), (map_hbm, map_ref),
        ))
    ]
    loads = [
        pltpu.make_async_copy(left_ref, held.at[pl.ds(0, rows)], load_sem.at[0]),
        pltpu.make_async_copy(right_ref, held.at[pl.ds(rows, rows)], load_sem.at[1]),
    ]
    for load in small + loads:
        load.start()
    for load in small:
        load.wait()

    raw[side, grp, 2] = kinds_ref[...].astype(F32)
    low_digit = lax.broadcasted_iota(jnp.int32, (LOW, LANES), 0)
    high_digit = lax.broadcasted_iota(jnp.int32, (8, 8, LANES), 0).reshape(64, LANES) + 8 * grp

    def mark(r, _):
        own = perm_ref[pl.ds(r, 1), :]
        columns = pl.ds(pl.multiple_of(r * LANES, LANES), LANES)
        one_hot[:, columns] = jnp.where(own % LOW == low_digit, 1.0, 0.0).astype(BF16)
        spread[:, columns] = jnp.where(own // LOW == high_digit, 1.0, 0.0).astype(BF16)
        return 0

    lax.fori_loop(0, count // LANES, mark, 0, unroll=4)
    pieces[:, 7, :] = jnp.zeros_like(pieces[:, 7, :])

    pl.semaphore_wait(barrier, 64)

    def send(mine, k, chip, core):
        pltpu.make_async_remote_copy(
            src_ref=mine, dst_ref=mine, send_sem=send_sem.at[k], recv_sem=recv_sem.at[k],
            device_id=(core, chip), device_id_type=MESH,
        ).start()

    visit_chips(grp, lambda chip: send(raw.at[side, grp], 0, chip, side))
    gathered = pltpu.make_async_remote_copy(
        src_ref=raw.at[0, pl.ds(0, 63)], dst_ref=raw.at[0, pl.ds(0, 63)], send_sem=send_sem.at[0],
        recv_sem=recv_sem.at[0], device_id=(1 - side, grp), device_id_type=MESH,
    )
    gathered.wait_recv()

    cross = pltpu.make_async_remote_copy(
        src_ref=raw.at[side], dst_ref=raw.at[side], send_sem=send_sem.at[1], recv_sem=recv_sem.at[1],
        device_id=(1 - side, grp), device_id_type=MESH,
    )
    cross.start()

    def split(j, _):
        pole = raw[side, j, 0]
        coupling = raw[side, j, 1]
        kind = raw[side, j, 2]
        coef_u = jnp.where((kind == 1.0) | (kind == 2.0), coupling, 0.0)
        coef_v = jnp.where(kind >= 2.0, pole * coupling, 0.0)
        square = pole * pole
        high = square.astype(BF16).astype(F32)
        rest = square - high
        middle = rest.astype(BF16).astype(F32)
        u_high = coef_u.astype(BF16).astype(F32)
        v_high = coef_v.astype(BF16).astype(F32)
        for q, piece in enumerate((high, middle, rest - middle, u_high, coef_u - u_high, v_high, coef_v - v_high)):
            pieces[pl.ds(j * 4, 4), q, :] = piece
        return 0

    lax.fori_loop(0, groups, split, 0, unroll=8)
    looked = None
    for i in range(count // STRIP):
        columns = pl.ds(i * STRIP, STRIP)
        block = [pieces[i * (STRIP // LANES) + r] for r in range(STRIP // LANES)]
        wide = jnp.concatenate([jnp.concatenate([p, p], axis=0).astype(BF16) for p in block], axis=1)
        picked = jnp.concatenate([spread[pl.ds(16 * t, 16), columns] * wide for t in range(4)], axis=0)
        part = lax.dot_general(
            picked, one_hot[:, columns], (((1,), (1,)), ((), ())), preferred_element_type=F32
        )
        looked = part if looked is None else looked + part
    found[...] = looked
    digits = [
        jnp.concatenate([found[pl.ds(q + 8 * half, 4, stride=16), :] for half in range(2)], axis=1)
        for q in range(7)
    ]
    placed[grp, 0] = digits[0] + (digits[1] + digits[2])
    placed[grp, 1] = digits[3] + digits[4]
    placed[grp, 2] = digits[5] + digits[6]

    visit_chips(grp, lambda chip: send(placed.at[grp], 2, chip, side))

    cross.wait_recv()

    def lay_out(j, _):
        pole = jnp.concatenate([raw[0, j, 0], raw[1, j, 0]], axis=0)
        coupling = jnp.concatenate([raw[0, j, 1], raw[1, j, 1]], axis=0)
        kind = jnp.concatenate([raw[0, j, 2], raw[1, j, 2]], axis=0)
        sq[j] = pole * pole
        weight[j] = jnp.where(kind != 0.0, coupling, 0.0) * coupling
        return 0

    lax.fori_loop(0, groups, lay_out, 0, unroll=4)

    lane = lax.broadcasted_iota(jnp.int32, (1, LANES), 1)
    last = groups - 1

    def pick(row, at):
        return total(jnp.where(lane == at, row, 0.0))

    after = jnp.where(me == 127, 0, -1)
    first_low = pick(sq[last, 3:4], me)
    first_high = pick(sq[last, 3:4], me + 1) + pick(sq[0, 4:5], after)
    second_low = pick(sq[last, 6:7], me)
    second_high = pick(sq[last, 6:7], me + 1) + pick(sq[last, 7:8], after)
    lows = (first_low, second_low)
    gaps = (first_high - first_low, second_high - second_low)
    starts = tuple(low + 0.1 * gap for low, gap in zip(lows, gaps))
    ends = tuple(high - 0.1 * gap for high, gap in zip((first_high, second_high), gaps))
    blocks = 8

    def visit(shifts, extra):
        zero = jnp.zeros((8, LANES), F32)
        sums = [[zero, zero], [zero, zero]]
        wide = [jnp.broadcast_to(shift, (8, LANES)) for shift in shifts]
        for b in range(groups // blocks):
            at = pl.ds(b * blocks, blocks)
            sq_block = sq[at]
            lead, tail = extra(at, sq_block)
            for k in range(2):
                inverse = recip(sq_block - wide[k])
                if lead is None:
                    part = tail * inverse
                    sums[k][0] = sums[k][0] + jnp.sum(part, axis=0)
                    sums[k][1] = sums[k][1] + jnp.sum(part * inverse, axis=0)
                else:
                    squared = inverse * inverse
                    sums[k][0] = sums[k][0] + jnp.sum(lead * squared, axis=0)
                    sums[k][1] = sums[k][1] + jnp.sum(tail * squared, axis=0)
        stack = jnp.concatenate([jnp.sum(s, axis=0, keepdims=True) for pair in sums for s in pair], axis=0)
        stack = jnp.sum(stack, axis=1, keepdims=True)
        return [[stack[2 * k + n:2 * k + n + 1] for n in range(2)] for k in range(2)]

    def step(_, shifts):
        sums = visit(shifts, lambda at, sq_block: (None, weight[at]))
        return tuple(
            jnp.clip(shift - 0.5 * (1.0 + value) / slope, start, end)
            for shift, (value, slope), start, end in zip(shifts, sums, starts, ends)
        )

    shifts = lax.fori_loop(
        0, ITERS, step, tuple(low + 0.5 * gap for low, gap in zip(lows, gaps))
    )

    def norm_weights(at, sq_block):
        kind = jnp.concatenate([raw[0, at, 2], raw[1, at, 2]], axis=1)
        both = weight[at]
        return (
            jnp.where((kind == 1.0) | (kind == 2.0), both, 0.0),
            jnp.where(kind >= 2.0, sq_block * both, 0.0),
        )

    norms = visit(shifts, norm_weights)
    values = [shifts[0], shifts[1]]
    values += [lax.rsqrt(norms[k][0]) for k in range(2)]
    values += [lax.rsqrt(1.0 + norms[k][1]) for k in range(2)]
    values += [(shift - low) / gap for shift, low, gap in zip(shifts, lows, gaps)]
    row = jnp.zeros((1, LANES), F32)
    for k, value in enumerate(values):
        row = jnp.where(lane == k, value, row)
    answers[me] = row

    def send_answer(chip):
        for core in (side, 1 - side):
            send(answers.at[me], 3, chip, core)

    visit_chips(grp, send_answer)
    send(answers.at[me], 3, grp, 1 - side)

    for load in loads:
        load.wait()
    placing = pltpu.make_async_remote_copy(
        src_ref=placed.at[pl.ds(0, 63)], dst_ref=placed.at[pl.ds(0, 63)], send_sem=send_sem.at[2],
        recv_sem=recv_sem.at[2], device_id=(1 - side, grp), device_id_type=MESH,
    )
    placing.wait_recv()

    def spread_coefs(j, _):
        for h in range(4):
            columns = pl.ds(pl.multiple_of(j * 512 + h * LANES, LANES), LANES)
            for m in range(2):
                coef = jnp.where(map_ref[m, j * 2 + h // 2] != 0, placed[j, 1 + m, h:h + 1, :], 0.0)
                coefs[m, :, columns] = jnp.broadcast_to(coef, (16, LANES)).astype(BF16)
        return 0

    lax.fori_loop(0, groups, spread_coefs, 0)

    def scale(i, _):
        columns = pl.ds(pl.multiple_of(i * STRIP, STRIP), STRIP)
        for m in range(2):
            coef = coefs[m, :, columns]
            for t in range(rows // 16):
                part = pl.ds(m * rows + t * 16, 16)
                held[part, columns] = held[part, columns] * coef
        return 0

    lax.fori_loop(0, count // STRIP, scale, 0)
    acc[...] = jnp.zeros_like(acc)

    answered = pltpu.make_async_remote_copy(
        src_ref=answers.at[pl.ds(0, 127)], dst_ref=answers.at[pl.ds(0, 127)], send_sem=send_sem.at[3],
        recv_sem=recv_sem.at[3], device_id=(1 - side, grp), device_id_type=MESH,
    )
    answered.wait_recv()

    table = answers[:, 0, :]
    shift_cols[pl.ds(0, LANES)] = jnp.broadcast_to(table[:, 0:1], (LANES, LANES))
    shift_cols[pl.ds(LANES, LANES)] = jnp.broadcast_to(table[:, 1:2], (LANES, LANES))

    def fill(i, cauchy):
        shift = shift_cols[...]
        for j in range(CHUNK // 512):
            for h in range(4):
                difference = placed[i * (CHUNK // 512) + j, 0, h:h + 1, :] - shift
                cauchy[:, pl.ds(j * 512 + h * LANES, LANES)] = pl.reciprocal(difference, approx=True).astype(BF16)

    def multiply(i, cauchy):
        columns = pl.ds(pl.multiple_of(i * CHUNK, CHUNK), CHUNK)
        acc[...] += lax.dot_general(
            held[:, columns], cauchy[...], (((1,), (1,)), ((), ())), preferred_element_type=F32
        )

    chunks = count // CHUNK
    fill(0, cauchy_a)

    def pair(i, _):
        fill(2 * i + 1, cauchy_b)
        multiply(2 * i, cauchy_a)
        fill((2 * i + 2) % chunks, cauchy_a)
        multiply(2 * i + 1, cauchy_b)
        return 0

    lax.fori_loop(0, chunks // 2, pair, 0)
    turned = table.T
    norm_u = jnp.concatenate([turned[2:3], turned[3:4]], axis=1)
    norm_v = jnp.concatenate([turned[4:5], turned[5:6]], axis=1)
    out_left[...] = (acc[pl.ds(0, rows)] * norm_u).astype(BF16)
    out_right[...] = (acc[pl.ds(rows, rows)] * norm_v).astype(BF16)
    out_offsets[...] = turned[6:8]
    gathered.wait_send()
    cross.wait_send()
    placing.wait_send()
    answered.wait_send()


def hand_over(left_ref, right_ref, offsets_ref, out_left, out_right, out_offsets):
    out_left[...] = left_ref[...]
    out_right[...] = right_ref[...]
    out_offsets[...] = offsets_ref[...]


def on_device(poles, coupling, kinds, permutation, block_map, left_vectors, right_vectors):
    rows, count = left_vectors.shape[1:]
    own = poles.shape[0] // LANES
    groups = lax.axis_size("grp")
    vmem = pl.BlockSpec(memory_space=pltpu.VMEM)
    anywhere = pl.BlockSpec(memory_space=pl.ANY)
    left, right, offsets = pl.pallas_call(
        merge_kernel,
        out_shape=(
            jax.ShapeDtypeStruct((rows, 2 * LANES), BF16),
            jax.ShapeDtypeStruct((rows, 2 * LANES), BF16),
            jax.ShapeDtypeStruct((2, LANES), F32),
        ),
        in_specs=[anywhere] * 7,
        out_specs=(vmem, vmem, vmem),
        scratch_shapes=[
            pltpu.VMEM((count // LANES, LANES), jnp.int32),
            pltpu.VMEM((own, LANES), jnp.int32),
            pltpu.SMEM(block_map.shape[2:], jnp.int32),
            pltpu.VMEM((2 * rows, count), BF16),
            pltpu.VMEM((2, groups, 3, own, LANES), F32),
            pltpu.VMEM((LOW, count), BF16),
            pltpu.VMEM((count // LANES, 8, LANES), F32),
            pltpu.VMEM((64, count), BF16),
            pltpu.VMEM((64, LOW), F32),
            pltpu.VMEM((groups, 3, own, LANES), F32),
            pltpu.VMEM((groups, 8, LANES), F32),
            pltpu.VMEM((groups, 8, LANES), F32),
            pltpu.VMEM((2 * groups, 1, LANES), F32),
            pltpu.VMEM((2 * LANES, LANES), F32),
            pltpu.VMEM((2, 16, count), BF16),
            pltpu.VMEM((2 * LANES, CHUNK), BF16),
            pltpu.VMEM((2 * LANES, CHUNK), BF16),
            pltpu.VMEM((2 * rows, 2 * LANES), F32),
            pltpu.SemaphoreType.DMA((7,)),
            pltpu.SemaphoreType.DMA((4,)),
            pltpu.SemaphoreType.DMA((4,)),
        ],
        compiler_params=pltpu.CompilerParams(
            collective_id=0, has_side_effects=True, vmem_limit_bytes=58 * 2**20
        ),
    )(
        poles.reshape(own, LANES),
        coupling.reshape(own, LANES),
        kinds.reshape(own, LANES),
        permutation.reshape(count // LANES, LANES),
        block_map[0, 0],
        left_vectors[0],
        right_vectors[0],
    )
    left, right, offsets = pl.pallas_call(
        hand_over,
        out_shape=(
            jax.ShapeDtypeStruct(left.shape, BF16),
            jax.ShapeDtypeStruct(right.shape, BF16),
            jax.ShapeDtypeStruct(offsets.shape, F32),
        ),
        in_specs=[vmem] * 3,
        out_specs=(vmem,) * 3,
    )(left, right, offsets)
    return left[None], right[None], offsets.reshape(2 * LANES)


def solution(mesh):
    return jax.shard_map(
        on_device,
        mesh=mesh,
        in_specs=(
            P(("side", "grp")),
            P(("side", "grp")),
            P(("side", "grp")),
            P("side", None),
            P("side", "grp", None, None),
            P("side", "grp", None),
            P("side", "grp", None),
        ),
        out_specs=(P("side", "grp", None), P("side", "grp", None), P()),
        check_vma=False,
    )
```

```python
import functools

import jax
import jax.numpy as jnp
from jax import lax
from jax.experimental import pallas as pl
from jax.experimental.pallas import tpu as pltpu
from jax.sharding import PartitionSpec as P

MESH = pl.DeviceIdType.MESH
ITERS = 8
LANES = 128
BW = 256
LOW = 64
CHUNK = 4096
STRIP = 1024
WIDE = 2048
F32 = jnp.float32
BF16 = jnp.bfloat16


def visit_chips(grp, act):
    far_first = (2, 3, 1, 0)
    x, rest = lax.div(grp, 16), lax.rem(grp, 16)
    y, z = lax.div(rest, 4), lax.rem(rest, 4)
    xs = [16 * lax.rem(x + far, 4) for far in far_first]
    ys = [4 * lax.rem(y + far, 4) for far in far_first]
    zs = [lax.rem(z + far, 4) for far in far_first]
    for i in range(63):
        act(xs[i // 16] + ys[i // 4 % 4] + zs[i % 4])


def recip(value):
    guess = pl.reciprocal(value, approx=True)
    return guess + guess * (1.0 - value * guess)


def total(value):
    return jnp.sum(value, axis=(0, 1), keepdims=True)


def merge_kernel(
    poles_ref, coupling_ref, kinds_hbm, perm_hbm, map_hbm, left_ref, right_ref,
    out_left, out_right, out_offsets,
    perm_ref, kinds_ref, map_ref, held, raw, one_hot, pieces, spread, found, placed, sq, weight, answers,
    shift_cols, cauchy_a, cauchy_b, acc, load_sem, send_sem, recv_sem,
):
    side = lax.axis_index("side")
    grp = lax.axis_index("grp")
    me = side * 64 + grp
    rows = left_ref.shape[0]
    count = left_ref.shape[1]
    groups = raw.shape[1]

    barrier = pltpu.get_barrier_semaphore()

    def greet(chip, core):
        pl.semaphore_signal(barrier, inc=1, device_id=(core, chip), device_id_type=MESH)

    visit_chips(grp, lambda chip: greet(chip, side))
    greet(grp, 1 - side)

    small = [
        pltpu.make_async_copy(source, target, load_sem.at[2 + k])
        for k, (source, target) in enumerate((
            (perm_hbm, perm_ref), (poles_ref, raw.at[side, grp, 0]), (coupling_ref, raw.at[side, grp, 1]),
            (kinds_hbm, kinds_ref), (map_hbm, map_ref),
        ))
    ]
    loads = [
        pltpu.make_async_copy(left_ref, held.at[pl.ds(0, rows)], load_sem.at[0]),
        pltpu.make_async_copy(right_ref, held.at[pl.ds(rows, rows)], load_sem.at[1]),
    ]
    for load in small + loads:
        load.start()
    for load in small:
        load.wait()

    raw[side, grp, 2] = kinds_ref[...].astype(F32)
    low_digit = lax.broadcasted_iota(jnp.int32, (LOW, LANES), 0)
    high_digit = lax.broadcasted_iota(jnp.int32, (8, 8, LANES), 0).reshape(64, LANES) + 8 * grp

    def mark(r, _):
        own = perm_ref[pl.ds(r, 1), :]
        columns = pl.ds(pl.multiple_of(r * LANES, LANES), LANES)
        one_hot[:, columns] = jnp.where(own % LOW == low_digit, 1.0, 0.0).astype(BF16)
        spread[:, columns] = jnp.where(own // LOW == high_digit, 1.0, 0.0).astype(BF16)
        return 0

    lax.fori_loop(0, count // LANES, mark, 0, unroll=4)
    pieces[:, 7, :] = jnp.zeros_like(pieces[:, 7, :])

    pl.semaphore_wait(barrier, 64)

    def send(mine, k, chip, core):
        pltpu.make_async_remote_copy(
            src_ref=mine, dst_ref=mine, send_sem=send_sem.at[k], recv_sem=recv_sem.at[k],
            device_id=(core, chip), device_id_type=MESH,
        ).start()

    visit_chips(grp, lambda chip: send(raw.at[side, grp], 0, chip, side))
    gathered = pltpu.make_async_remote_copy(
        src_ref=raw.at[0, pl.ds(0, 63)], dst_ref=raw.at[0, pl.ds(0, 63)], send_sem=send_sem.at[0],
        recv_sem=recv_sem.at[0], device_id=(1 - side, grp), device_id_type=MESH,
    )
    gathered.wait_recv()

    cross = pltpu.make_async_remote_copy(
        src_ref=raw.at[side], dst_ref=raw.at[side], send_sem=send_sem.at[1], recv_sem=recv_sem.at[1],
        device_id=(1 - side, grp), device_id_type=MESH,
    )
    cross.start()

    def split(j, _):
        pole = raw[side, j, 0]
        coupling = raw[side, j, 1]
        kind = raw[side, j, 2]
        coef_u = jnp.where((kind == 1.0) | (kind == 2.0), coupling, 0.0)
        coef_v = jnp.where(kind >= 2.0, pole * coupling, 0.0)
        square = pole * pole
        high = square.astype(BF16).astype(F32)
        rest = square - high
        middle = rest.astype(BF16).astype(F32)
        u_high = coef_u.astype(BF16).astype(F32)
        v_high = coef_v.astype(BF16).astype(F32)
        for q, piece in enumerate((high, middle, rest - middle, u_high, coef_u - u_high, v_high, coef_v - v_high)):
            pieces[pl.ds(j * 4, 4), q, :] = piece
        return 0

    lax.fori_loop(0, groups, split, 0, unroll=8)
    looked = None
    for i in range(count // STRIP):
        columns = pl.ds(i * STRIP, STRIP)
        block = [pieces[i * (STRIP // LANES) + r] for r in range(STRIP // LANES)]
        wide = jnp.concatenate([jnp.concatenate([p, p], axis=0).astype(BF16) for p in block], axis=1)
        picked = jnp.concatenate([spread[pl.ds(16 * t, 16), columns] * wide for t in range(4)], axis=0)
        part = lax.dot_general(
            picked, one_hot[:, columns], (((1,), (1,)), ((), ())), preferred_element_type=F32
        )
        looked = part if looked is None else looked + part
    found[...] = looked
    digits = [
        jnp.concatenate([found[pl.ds(q + 8 * half, 4, stride=16), :] for half in range(2)], axis=1)
        for q in range(7)
    ]
    placed[grp, 0] = digits[0] + (digits[1] + digits[2])
    placed[grp, 1] = digits[3] + digits[4]
    placed[grp, 2] = digits[5] + digits[6]

    visit_chips(grp, lambda chip: send(placed.at[grp], 2, chip, side))

    cross.wait_recv()

    def lay_out(j, _):
        pole = jnp.concatenate([raw[0, j, 0], raw[1, j, 0]], axis=0)
        coupling = jnp.concatenate([raw[0, j, 1], raw[1, j, 1]], axis=0)
        kind = jnp.concatenate([raw[0, j, 2], raw[1, j, 2]], axis=0)
        sq[j] = pole * pole
        weight[j] = jnp.where(kind != 0.0, coupling, 0.0) * coupling
        return 0

    lax.fori_loop(0, groups, lay_out, 0, unroll=4)

    lane = lax.broadcasted_iota(jnp.int32, (1, LANES), 1)
    last = groups - 1

    def pick(row, at):
        return total(jnp.where(lane == at, row, 0.0))

    after = jnp.where(me == 127, 0, -1)
    first_low = pick(sq[last, 3:4], me)
    first_high = pick(sq[last, 3:4], me + 1) + pick(sq[0, 4:5], after)
    second_low = pick(sq[last, 6:7], me)
    second_high = pick(sq[last, 6:7], me + 1) + pick(sq[last, 7:8], after)
    lows = (first_low, second_low)
    gaps = (first_high - first_low, second_high - second_low)
    starts = tuple(low + 0.1 * gap for low, gap in zip(lows, gaps))
    ends = tuple(high - 0.1 * gap for high, gap in zip((first_high, second_high), gaps))
    blocks = 8

    def visit(shifts, extra):
        zero = jnp.zeros((8, LANES), F32)
        sums = [[zero, zero], [zero, zero]]
        wide = [jnp.broadcast_to(shift, (8, LANES)) for shift in shifts]
        for b in range(groups // blocks):
            at = pl.ds(b * blocks, blocks)
            sq_block = sq[at]
            lead, tail = extra(at, sq_block)
            for k in range(2):
                inverse = recip(sq_block - wide[k])
                if lead is None:
                    part = tail * inverse
                    sums[k][0] = sums[k][0] + jnp.sum(part, axis=0)
                    sums[k][1] = sums[k][1] + jnp.sum(part * inverse, axis=0)
                else:
                    squared = inverse * inverse
                    sums[k][0] = sums[k][0] + jnp.sum(lead * squared, axis=0)
                    sums[k][1] = sums[k][1] + jnp.sum(tail * squared, axis=0)
        stack = jnp.concatenate([jnp.sum(s, axis=0, keepdims=True) for pair in sums for s in pair], axis=0)
        stack = jnp.sum(stack, axis=1, keepdims=True)
        return [[stack[2 * k + n:2 * k + n + 1] for n in range(2)] for k in range(2)]

    def step(_, shifts):
        sums = visit(shifts, lambda at, sq_block: (None, weight[at]))
        return tuple(
            jnp.clip(shift - 0.5 * (1.0 + value) / slope, start, end)
            for shift, (value, slope), start, end in zip(shifts, sums, starts, ends)
        )

    shifts = lax.fori_loop(
        0, ITERS, step, tuple(low + 0.5 * gap for low, gap in zip(lows, gaps))
    )

    def norm_weights(at, sq_block):
        kind = jnp.concatenate([raw[0, at, 2], raw[1, at, 2]], axis=1)
        both = weight[at]
        return (
            jnp.where((kind == 1.0) | (kind == 2.0), both, 0.0),
            jnp.where(kind >= 2.0, sq_block * both, 0.0),
        )

    norms = visit(shifts, norm_weights)
    values = [shifts[0], shifts[1]]
    values += [lax.rsqrt(norms[k][0]) for k in range(2)]
    values += [lax.rsqrt(1.0 + norms[k][1]) for k in range(2)]
    values += [(shift - low) / gap for shift, low, gap in zip(shifts, lows, gaps)]
    row = jnp.zeros((1, LANES), F32)
    for k, value in enumerate(values):
        row = jnp.where(lane == k, value, row)
    answers[me] = row

    def send_answer(chip):
        for core in (side, 1 - side):
            send(answers.at[me], 3, chip, core)

    visit_chips(grp, send_answer)
    send(answers.at[me], 3, grp, 1 - side)

    for load in loads:
        load.wait()
    placing = pltpu.make_async_remote_copy(
        src_ref=placed.at[pl.ds(0, 63)], dst_ref=placed.at[pl.ds(0, 63)], send_sem=send_sem.at[2],
        recv_sem=recv_sem.at[2], device_id=(1 - side, grp), device_id_type=MESH,
    )
    placing.wait_recv()

    def scale(i, _):
        columns = pl.ds(pl.multiple_of(i * WIDE, WIDE), WIDE)
        for m in range(2):
            line = []
            for k in range(WIDE // BW):
                keep = map_ref[m, i * (WIDE // BW) + k] != 0
                for h in (2 * k, 2 * k + 1):
                    coef = placed[i * (WIDE // 512) + h // 4, 1 + m, h % 4:h % 4 + 1, :]
                    line.append(jnp.where(keep, coef, 0.0))
            coef = jnp.broadcast_to(jnp.concatenate(line, axis=1), (16, WIDE)).astype(BF16)
            for t in range(rows // 16):
                part = pl.ds(m * rows + t * 16, 16)
                held[part, columns] = held[part, columns] * coef
        return 0

    lax.fori_loop(0, count // WIDE, scale, 0)
    acc[...] = jnp.zeros_like(acc)

    answered = pltpu.make_async_remote_copy(
        src_ref=answers.at[pl.ds(0, 127)], dst_ref=answers.at[pl.ds(0, 127)], send_sem=send_sem.at[3],
        recv_sem=recv_sem.at[3], device_id=(1 - side, grp), device_id_type=MESH,
    )
    answered.wait_recv()

    table = answers[:, 0, :]
    shift_cols[pl.ds(0, LANES)] = jnp.broadcast_to(table[:, 0:1], (LANES, LANES))
    shift_cols[pl.ds(LANES, LANES)] = jnp.broadcast_to(table[:, 1:2], (LANES, LANES))

    def fill(i, cauchy):
        shift = shift_cols[...]
        for j in range(CHUNK // 512):
            for h in range(4):
                difference = placed[i * (CHUNK // 512) + j, 0, h:h + 1, :] - shift
                cauchy[:, pl.ds(j * 512 + h * LANES, LANES)] = pl.reciprocal(difference, approx=True).astype(BF16)

    def multiply(i, cauchy):
        columns = pl.ds(pl.multiple_of(i * CHUNK, CHUNK), CHUNK)
        acc[...] += lax.dot_general(
            held[:, columns], cauchy[...], (((1,), (1,)), ((), ())), preferred_element_type=F32
        )

    chunks = count // CHUNK
    fill(0, cauchy_a)

    def pair(i, _):
        fill(2 * i + 1, cauchy_b)
        multiply(2 * i, cauchy_a)
        fill((2 * i + 2) % chunks, cauchy_a)
        multiply(2 * i + 1, cauchy_b)
        return 0

    lax.fori_loop(0, chunks // 2, pair, 0)
    turned = table.T
    norm_u = jnp.concatenate([turned[2:3], turned[3:4]], axis=1)
    norm_v = jnp.concatenate([turned[4:5], turned[5:6]], axis=1)
    out_left[...] = (acc[pl.ds(0, rows)] * norm_u).astype(BF16)
    out_right[...] = (acc[pl.ds(rows, rows)] * norm_v).astype(BF16)
    out_offsets[...] = turned[6:8]
    gathered.wait_send()
    cross.wait_send()
    placing.wait_send()
    answered.wait_send()


def hand_over(left_ref, right_ref, offsets_ref, out_left, out_right, out_offsets):
    out_left[...] = left_ref[...]
    out_right[...] = right_ref[...]
    out_offsets[...] = offsets_ref[...]


def on_device(poles, coupling, kinds, permutation, block_map, left_vectors, right_vectors):
    rows, count = left_vectors.shape[1:]
    own = poles.shape[0] // LANES
    groups = lax.axis_size("grp")
    vmem = pl.BlockSpec(memory_space=pltpu.VMEM)
    anywhere = pl.BlockSpec(memory_space=pl.ANY)
    left, right, offsets = pl.pallas_call(
        merge_kernel,
        out_shape=(
            jax.ShapeDtypeStruct((rows, 2 * LANES), BF16),
            jax.ShapeDtypeStruct((rows, 2 * LANES), BF16),
            jax.ShapeDtypeStruct((2, LANES), F32),
        ),
        in_specs=[anywhere] * 7,
        out_specs=(vmem, vmem, vmem),
        scratch_shapes=[
            pltpu.VMEM((count // LANES, LANES), jnp.int32),
            pltpu.VMEM((own, LANES), jnp.int32),
            pltpu.SMEM(block_map.shape[2:], jnp.int32),
            pltpu.VMEM((2 * rows, count), BF16),
            pltpu.VMEM((2, groups, 3, own, LANES), F32),
            pltpu.VMEM((LOW, count), BF16),
            pltpu.VMEM((count // LANES, 8, LANES), F32),
            pltpu.VMEM((64, count), BF16),
            pltpu.VMEM((64, LOW), F32),
            pltpu.VMEM((groups, 3, own, LANES), F32),
            pltpu.VMEM((groups, 8, LANES), F32),
            pltpu.VMEM((groups, 8, LANES), F32),
            pltpu.VMEM((2 * groups, 1, LANES), F32),
            pltpu.VMEM((2 * LANES, LANES), F32),
            pltpu.VMEM((2 * LANES, CHUNK), BF16),
            pltpu.VMEM((2 * LANES, CHUNK), BF16),
            pltpu.VMEM((2 * rows, 2 * LANES), F32),
            pltpu.SemaphoreType.DMA((7,)),
            pltpu.SemaphoreType.DMA((4,)),
            pltpu.SemaphoreType.DMA((4,)),
        ],
        compiler_params=pltpu.CompilerParams(
            collective_id=0, has_side_effects=True, vmem_limit_bytes=58 * 2**20
        ),
    )(
        poles.reshape(own, LANES),
        coupling.reshape(own, LANES),
        kinds.reshape(own, LANES),
        permutation.reshape(count // LANES, LANES),
        block_map[0, 0],
        left_vectors[0],
        right_vectors[0],
    )
    left, right, offsets = pl.pallas_call(
        hand_over,
        out_shape=(
            jax.ShapeDtypeStruct(left.shape, BF16),
            jax.ShapeDtypeStruct(right.shape, BF16),
            jax.ShapeDtypeStruct(offsets.shape, F32),
        ),
        in_specs=[vmem] * 3,
        out_specs=(vmem,) * 3,
    )(left, right, offsets)
    return left[None], right[None], offsets.reshape(2 * LANES)


def solution(mesh):
    return jax.shard_map(
        on_device,
        mesh=mesh,
        in_specs=(
            P(("side", "grp")),
            P(("side", "grp")),
            P(("side", "grp")),
            P("side", None),
            P("side", "grp", None, None),
            P("side", "grp", None),
            P("side", "grp", None),
        ),
        out_specs=(P("side", "grp", None), P("side", "grp", None), P()),
        check_vma=False,
    )
```

```python
import functools

import jax
import jax.numpy as jnp
from jax import lax
from jax.experimental import pallas as pl
from jax.experimental.pallas import tpu as pltpu
from jax.sharding import PartitionSpec as P

MESH = pl.DeviceIdType.MESH
ITERS = 8
LANES = 128
BW = 256
LOW = 64
CHUNK = 4096
STRIP = 1024
WIDE = 2048
F32 = jnp.float32
BF16 = jnp.bfloat16


def visit_chips(grp, act):
    far_first = (2, 3, 1, 0)
    x, rest = lax.div(grp, 16), lax.rem(grp, 16)
    y, z = lax.div(rest, 4), lax.rem(rest, 4)
    xs = [16 * lax.rem(x + far, 4) for far in far_first]
    ys = [4 * lax.rem(y + far, 4) for far in far_first]
    zs = [lax.rem(z + far, 4) for far in far_first]
    for i in range(63):
        act(xs[i // 16] + ys[i // 4 % 4] + zs[i % 4])


def recip(value):
    guess = pl.reciprocal(value, approx=True)
    return guess + guess * (1.0 - value * guess)


def total(value):
    return jnp.sum(value, axis=(0, 1), keepdims=True)


def merge_kernel(
    poles_ref, coupling_ref, kinds_hbm, perm_hbm, map_hbm, left_ref, right_ref,
    out_left, out_right, out_offsets,
    perm_ref, kinds_ref, map_ref, held, raw, one_hot, pieces, spread, found, placed, sq, weight, answers,
    shift_cols, cauchy_a, cauchy_b, acc, load_sem, send_sem, recv_sem,
):
    side = lax.axis_index("side")
    grp = lax.axis_index("grp")
    me = side * 64 + grp
    rows = left_ref.shape[0]
    count = left_ref.shape[1]
    groups = raw.shape[1]

    barrier = pltpu.get_barrier_semaphore()

    def greet(chip, core):
        pl.semaphore_signal(barrier, inc=1, device_id=(core, chip), device_id_type=MESH)

    visit_chips(grp, lambda chip: greet(chip, side))
    greet(grp, 1 - side)

    small = [
        pltpu.make_async_copy(source, target, load_sem.at[2 + k])
        for k, (source, target) in enumerate((
            (perm_hbm, perm_ref), (poles_ref, raw.at[side, grp, 0]), (coupling_ref, raw.at[side, grp, 1]),
            (kinds_hbm, kinds_ref), (map_hbm, map_ref),
        ))
    ]
    loads = [
        pltpu.make_async_copy(left_ref, held.at[pl.ds(0, rows)], load_sem.at[0]),
        pltpu.make_async_copy(right_ref, held.at[pl.ds(rows, rows)], load_sem.at[1]),
    ]
    for load in small + loads:
        load.start()
    for load in small:
        load.wait()

    raw[side, grp, 2] = kinds_ref[...].astype(F32)

    pl.semaphore_wait(barrier, 64)

    def send(mine, k, chip, core):
        pltpu.make_async_remote_copy(
            src_ref=mine, dst_ref=mine, send_sem=send_sem.at[k], recv_sem=recv_sem.at[k],
            device_id=(core, chip), device_id_type=MESH,
        ).start()

    visit_chips(grp, lambda chip: send(raw.at[side, grp], 0, chip, side))

    low_digit = lax.broadcasted_iota(jnp.int32, (LOW, LANES), 0)
    high_digit = lax.broadcasted_iota(jnp.int32, (8, 8, LANES), 0).reshape(64, LANES) + 8 * grp

    def mark(r, _):
        own = perm_ref[pl.ds(r, 1), :]
        columns = pl.ds(pl.multiple_of(r * LANES, LANES), LANES)
        one_hot[:, columns] = jnp.where(own % LOW == low_digit, 1.0, 0.0).astype(BF16)
        spread[:, columns] = jnp.where(own // LOW == high_digit, 1.0, 0.0).astype(BF16)
        return 0

    lax.fori_loop(0, count // LANES, mark, 0, unroll=4)
    pieces[:, 7, :] = jnp.zeros_like(pieces[:, 7, :])

    gathered = pltpu.make_async_remote_copy(
        src_ref=raw.at[0, pl.ds(0, 63)], dst_ref=raw.at[0, pl.ds(0, 63)], send_sem=send_sem.at[0],
        recv_sem=recv_sem.at[0], device_id=(1 - side, grp), device_id_type=MESH,
    )
    gathered.wait_recv()

    cross = pltpu.make_async_remote_copy(
        src_ref=raw.at[side], dst_ref=raw.at[side], send_sem=send_sem.at[1], recv_sem=recv_sem.at[1],
        device_id=(1 - side, grp), device_id_type=MESH,
    )
    cross.start()

    def split(j, _):
        pole = raw[side, j, 0]
        coupling = raw[side, j, 1]
        kind = raw[side, j, 2]
        coef_u = jnp.where((kind == 1.0) | (kind == 2.0), coupling, 0.0)
        coef_v = jnp.where(kind >= 2.0, pole * coupling, 0.0)
        square = pole * pole
        high = square.astype(BF16).astype(F32)
        rest = square - high
        middle = rest.astype(BF16).astype(F32)
        u_high = coef_u.astype(BF16).astype(F32)
        v_high = coef_v.astype(BF16).astype(F32)
        for q, piece in enumerate((high, middle, rest - middle, u_high, coef_u - u_high, v_high, coef_v - v_high)):
            pieces[pl.ds(j * 4, 4), q, :] = piece
        return 0

    lax.fori_loop(0, groups, split, 0, unroll=8)
    looked = None
    for i in range(count // STRIP):
        columns = pl.ds(i * STRIP, STRIP)
        block = [pieces[i * (STRIP // LANES) + r] for r in range(STRIP // LANES)]
        wide = jnp.concatenate([jnp.concatenate([p, p], axis=0).astype(BF16) for p in block], axis=1)
        picked = jnp.concatenate([spread[pl.ds(16 * t, 16), columns] * wide for t in range(4)], axis=0)
        part = lax.dot_general(
            picked, one_hot[:, columns], (((1,), (1,)), ((), ())), preferred_element_type=F32
        )
        looked = part if looked is None else looked + part
    found[...] = looked
    digits = [
        jnp.concatenate([found[pl.ds(q + 8 * half, 4, stride=16), :] for half in range(2)], axis=1)
        for q in range(7)
    ]
    placed[grp, 0] = digits[0] + (digits[1] + digits[2])
    placed[grp, 1] = digits[3] + digits[4]
    placed[grp, 2] = digits[5] + digits[6]

    visit_chips(grp, lambda chip: send(placed.at[grp], 2, chip, side))

    cross.wait_recv()

    def lay_out(j, _):
        pole = jnp.concatenate([raw[0, j, 0], raw[1, j, 0]], axis=0)
        coupling = jnp.concatenate([raw[0, j, 1], raw[1, j, 1]], axis=0)
        kind = jnp.concatenate([raw[0, j, 2], raw[1, j, 2]], axis=0)
        sq[j] = pole * pole
        weight[j] = jnp.where(kind != 0.0, coupling, 0.0) * coupling
        return 0

    lax.fori_loop(0, groups, lay_out, 0, unroll=4)

    lane = lax.broadcasted_iota(jnp.int32, (1, LANES), 1)
    last = groups - 1

    def pick(row, at):
        return total(jnp.where(lane == at, row, 0.0))

    after = jnp.where(me == 127, 0, -1)
    first_low = pick(sq[last, 3:4], me)
    first_high = pick(sq[last, 3:4], me + 1) + pick(sq[0, 4:5], after)
    second_low = pick(sq[last, 6:7], me)
    second_high = pick(sq[last, 6:7], me + 1) + pick(sq[last, 7:8], after)
    lows = (first_low, second_low)
    gaps = (first_high - first_low, second_high - second_low)
    starts = tuple(low + 0.1 * gap for low, gap in zip(lows, gaps))
    ends = tuple(high - 0.1 * gap for high, gap in zip((first_high, second_high), gaps))
    blocks = 8

    def visit(shifts, extra):
        zero = jnp.zeros((8, LANES), F32)
        sums = [[zero, zero], [zero, zero]]
        wide = [jnp.broadcast_to(shift, (8, LANES)) for shift in shifts]
        for b in range(groups // blocks):
            at = pl.ds(b * blocks, blocks)
            sq_block = sq[at]
            lead, tail = extra(at, sq_block)
            for k in range(2):
                inverse = recip(sq_block - wide[k])
                if lead is None:
                    part = tail * inverse
                    sums[k][0] = sums[k][0] + jnp.sum(part, axis=0)
                    sums[k][1] = sums[k][1] + jnp.sum(part * inverse, axis=0)
                else:
                    squared = inverse * inverse
                    sums[k][0] = sums[k][0] + jnp.sum(lead * squared, axis=0)
                    sums[k][1] = sums[k][1] + jnp.sum(tail * squared, axis=0)
        stack = jnp.concatenate([jnp.sum(s, axis=0, keepdims=True) for pair in sums for s in pair], axis=0)
        stack = jnp.sum(stack, axis=1, keepdims=True)
        return [[stack[2 * k + n:2 * k + n + 1] for n in range(2)] for k in range(2)]

    def step(_, shifts):
        sums = visit(shifts, lambda at, sq_block: (None, weight[at]))
        return tuple(
            jnp.clip(shift - 0.5 * (1.0 + value) / slope, start, end)
            for shift, (value, slope), start, end in zip(shifts, sums, starts, ends)
        )

    shifts = lax.fori_loop(
        0, ITERS, step, tuple(low + 0.5 * gap for low, gap in zip(lows, gaps))
    )

    def norm_weights(at, sq_block):
        kind = jnp.concatenate([raw[0, at, 2], raw[1, at, 2]], axis=1)
        both = weight[at]
        return (
            jnp.where((kind == 1.0) | (kind == 2.0), both, 0.0),
            jnp.where(kind >= 2.0, sq_block * both, 0.0),
        )

    norms = visit(shifts, norm_weights)
    values = [shifts[0], shifts[1]]
    values += [lax.rsqrt(norms[k][0]) for k in range(2)]
    values += [lax.rsqrt(1.0 + norms[k][1]) for k in range(2)]
    values += [(shift - low) / gap for shift, low, gap in zip(shifts, lows, gaps)]
    row = jnp.zeros((1, LANES), F32)
    for k, value in enumerate(values):
        row = jnp.where(lane == k, value, row)
    answers[me] = row

    def send_answer(chip):
        for core in (side, 1 - side):
            send(answers.at[me], 3, chip, core)

    visit_chips(grp, send_answer)
    send(answers.at[me], 3, grp, 1 - side)

    for load in loads:
        load.wait()
    placing = pltpu.make_async_remote_copy(
        src_ref=placed.at[pl.ds(0, 63)], dst_ref=placed.at[pl.ds(0, 63)], send_sem=send_sem.at[2],
        recv_sem=recv_sem.at[2], device_id=(1 - side, grp), device_id_type=MESH,
    )
    placing.wait_recv()

    def scale(i, _):
        columns = pl.ds(pl.multiple_of(i * WIDE, WIDE), WIDE)
        for m in range(2):
            line = []
            for k in range(WIDE // BW):
                keep = map_ref[m, i * (WIDE // BW) + k] != 0
                for h in (2 * k, 2 * k + 1):
                    coef = placed[i * (WIDE // 512) + h // 4, 1 + m, h % 4:h % 4 + 1, :]
                    line.append(jnp.where(keep, coef, 0.0))
            coef = jnp.broadcast_to(jnp.concatenate(line, axis=1), (16, WIDE)).astype(BF16)
            for t in range(rows // 16):
                part = pl.ds(m * rows + t * 16, 16)
                held[part, columns] = held[part, columns] * coef
        return 0

    lax.fori_loop(0, count // WIDE, scale, 0)
    acc[...] = jnp.zeros_like(acc)

    answered = pltpu.make_async_remote_copy(
        src_ref=answers.at[pl.ds(0, 127)], dst_ref=answers.at[pl.ds(0, 127)], send_sem=send_sem.at[3],
        recv_sem=recv_sem.at[3], device_id=(1 - side, grp), device_id_type=MESH,
    )
    answered.wait_recv()

    table = answers[:, 0, :]
    shift_cols[pl.ds(0, LANES)] = jnp.broadcast_to(table[:, 0:1], (LANES, LANES))
    shift_cols[pl.ds(LANES, LANES)] = jnp.broadcast_to(table[:, 1:2], (LANES, LANES))

    def fill(i, cauchy):
        shift = shift_cols[...]
        for j in range(CHUNK // 512):
            for h in range(4):
                difference = placed[i * (CHUNK // 512) + j, 0, h:h + 1, :] - shift
                cauchy[:, pl.ds(j * 512 + h * LANES, LANES)] = pl.reciprocal(difference, approx=True).astype(BF16)

    def multiply(i, cauchy):
        columns = pl.ds(pl.multiple_of(i * CHUNK, CHUNK), CHUNK)
        acc[...] += lax.dot_general(
            held[:, columns], cauchy[...], (((1,), (1,)), ((), ())), preferred_element_type=F32
        )

    chunks = count // CHUNK
    fill(0, cauchy_a)

    def pair(i, _):
        fill(2 * i + 1, cauchy_b)
        multiply(2 * i, cauchy_a)
        fill((2 * i + 2) % chunks, cauchy_a)
        multiply(2 * i + 1, cauchy_b)
        return 0

    lax.fori_loop(0, chunks // 2, pair, 0)
    turned = table.T
    norm_u = jnp.concatenate([turned[2:3], turned[3:4]], axis=1)
    norm_v = jnp.concatenate([turned[4:5], turned[5:6]], axis=1)
    out_left[...] = (acc[pl.ds(0, rows)] * norm_u).astype(BF16)
    out_right[...] = (acc[pl.ds(rows, rows)] * norm_v).astype(BF16)
    out_offsets[...] = turned[6:8]
    gathered.wait_send()
    cross.wait_send()
    placing.wait_send()
    answered.wait_send()


def hand_over(left_ref, right_ref, offsets_ref, out_left, out_right, out_offsets):
    out_left[...] = left_ref[...]
    out_right[...] = right_ref[...]
    out_offsets[...] = offsets_ref[...]


def on_device(poles, coupling, kinds, permutation, block_map, left_vectors, right_vectors):
    rows, count = left_vectors.shape[1:]
    own = poles.shape[0] // LANES
    groups = lax.axis_size("grp")
    vmem = pl.BlockSpec(memory_space=pltpu.VMEM)
    anywhere = pl.BlockSpec(memory_space=pl.ANY)
    left, right, offsets = pl.pallas_call(
        merge_kernel,
        out_shape=(
            jax.ShapeDtypeStruct((rows, 2 * LANES), BF16),
            jax.ShapeDtypeStruct((rows, 2 * LANES), BF16),
            jax.ShapeDtypeStruct((2, LANES), F32),
        ),
        in_specs=[anywhere] * 7,
        out_specs=(vmem, vmem, vmem),
        scratch_shapes=[
            pltpu.VMEM((count // LANES, LANES), jnp.int32),
            pltpu.VMEM((own, LANES), jnp.int32),
            pltpu.SMEM(block_map.shape[2:], jnp.int32),
            pltpu.VMEM((2 * rows, count), BF16),
            pltpu.VMEM((2, groups, 3, own, LANES), F32),
            pltpu.VMEM((LOW, count), BF16),
            pltpu.VMEM((count // LANES, 8, LANES), F32),
            pltpu.VMEM((64, count), BF16),
            pltpu.VMEM((64, LOW), F32),
            pltpu.VMEM((groups, 3, own, LANES), F32),
            pltpu.VMEM((groups, 8, LANES), F32),
            pltpu.VMEM((groups, 8, LANES), F32),
            pltpu.VMEM((2 * groups, 1, LANES), F32),
            pltpu.VMEM((2 * LANES, LANES), F32),
            pltpu.VMEM((2 * LANES, CHUNK), BF16),
            pltpu.VMEM((2 * LANES, CHUNK), BF16),
            pltpu.VMEM((2 * rows, 2 * LANES), F32),
            pltpu.SemaphoreType.DMA((7,)),
            pltpu.SemaphoreType.DMA((4,)),
            pltpu.SemaphoreType.DMA((4,)),
        ],
        compiler_params=pltpu.CompilerParams(
            collective_id=0, has_side_effects=True, vmem_limit_bytes=58 * 2**20
        ),
    )(
        poles.reshape(own, LANES),
        coupling.reshape(own, LANES),
        kinds.reshape(own, LANES),
        permutation.reshape(count // LANES, LANES),
        block_map[0, 0],
        left_vectors[0],
        right_vectors[0],
    )
    left, right, offsets = pl.pallas_call(
        hand_over,
        out_shape=(
            jax.ShapeDtypeStruct(left.shape, BF16),
            jax.ShapeDtypeStruct(right.shape, BF16),
            jax.ShapeDtypeStruct(offsets.shape, F32),
        ),
        in_specs=[vmem] * 3,
        out_specs=(vmem,) * 3,
    )(left, right, offsets)
    return left[None], right[None], offsets.reshape(2 * LANES)


def solution(mesh):
    return jax.shard_map(
        on_device,
        mesh=mesh,
        in_specs=(
            P(("side", "grp")),
            P(("side", "grp")),
            P(("side", "grp")),
            P("side", None),
            P("side", "grp", None, None),
            P("side", "grp", None),
            P("side", "grp", None),
        ),
        out_specs=(P("side", "grp", None), P("side", "grp", None), P()),
        check_vma=False,
    )
```
